512 devices in a mesh: frame: 16 (over x, y_lo, core), clip: 32 (over y_hi, z).
Axes of the slice: x: 4, y: 4 (y_hi: 2, y_lo: 2; y = y_hi * 2 + y_lo), z: 16, core: 2. Of those that a mesh axis runs over, the one named last changes fastest.
Arguments:
- within_frame_asker_matrix: bfloat16 [32, 16, 128, 1536], P('clip', 'frame'), may hold values from -400 to 400
- within_frame_matcher_matrix: bfloat16 [32, 16, 128, 1536], P('clip', 'frame'), may hold values from -6 to 6
- within_frame_payload_matrix: bfloat16 [32, 16, 128, 1536], P('clip', 'frame'), may hold values from -5 to 5
- within_frame_upstream_derivative: bfloat16 [32, 16, 128, 1536], P('clip', 'frame'), may hold values from -48 to 48
- across_time_asker_matrix: bfloat16 [32, 16, 128, 1536], P('clip', 'frame'), may hold values from -400 to 400
- across_time_matcher_matrix: bfloat16 [32, 16, 128, 1536], P('clip', 'frame'), may hold values from -6 to 6
- across_time_payload_matrix: bfloat16 [32, 16, 128, 1536], P('clip', 'frame'), may hold values from -5 to 5
- across_time_upstream_derivative: bfloat16 [32, 16, 128, 1536], P('clip', 'frame'), may hold values from -48 to 48
- sharpness_factor: float32 [2, 12], replicated, may hold values from 0.7 to 1.4
Outputs:
- spatial_query_grad: bfloat16 [32, 16, 128, 1536], P('clip', 'frame')
- spatial_key_grad: bfloat16 [32, 16, 128, 1536], P('clip', 'frame')
- temporal_query_grad: bfloat16 [32, 16, 128, 1536], P('clip', 'frame')
- temporal_key_grad: bfloat16 [32, 16, 128, 1536], P('clip', 'frame')
- temporal_value_grad: bfloat16 [32, 16, 128, 1536], P('clip', 'frame')
- logit_scale_gradient: float32 [2, 12], replicated
The draws below stay inside these ranges and needn't reach their ends.
All inputs are finite; a program needn't handle non-finite values.
Results may differ from the reference program's by a relative error of at most 0.011.
Values may be sent and summed in bfloat16 or wider, within the bound.
No kernel may reach another device: no remote copies, remote signals or barrier semaphores. Data moves between devices by JAX's collectives and lax.ppermute only.
A program may use at most 64 MiB of HBM per device.

```python
import math
import jax
import jax.numpy as jnp
from jax import lax

SHARD_CHANNELS = 12
K = 128
PATCHES = 128
FRAMES = 16
CLIPS = 32


def clipped_normal(key, full_shape):
    return jnp.clip(jax.random.normal(key, full_shape, jnp.float32), -5.0, 5.0)


def spatial_common(key):
    return clipped_normal(key, (CLIPS, FRAMES, PATCHES, SHARD_CHANNELS * K))


def temporal_common(key):
    return clipped_normal(jax.random.fold_in(key, 101), (CLIPS, FRAMES, PATCHES, SHARD_CHANNELS * K))


def rising_scale():
    clip_pos = jnp.arange(CLIPS, dtype=jnp.float32) / max(CLIPS - 1, 1)
    frame_pos = jnp.arange(FRAMES, dtype=jnp.float32) / max(FRAMES - 1, 1)
    return jnp.exp(math.log(3.0) * (clip_pos[:, None] + frame_pos[None, :]))[:, :, None, None]


def draw_within_frame_asker_matrix(key, part):
    key = jax.random.fold_in(key, 5)
    full_shape = (CLIPS, FRAMES, PATCHES, SHARD_CHANNELS * K)
    return clipped_normal(key, full_shape).astype(jnp.bfloat16)


def draw_within_frame_matcher_matrix(key, part):
    common = spatial_common(key)
    return common.astype(jnp.bfloat16)


def draw_across_time_asker_matrix(key, part):
    key = jax.random.fold_in(key, 13)
    full_shape = (CLIPS, FRAMES, PATCHES, SHARD_CHANNELS * K)
    return clipped_normal(key, full_shape).astype(jnp.bfloat16)


def draw_across_time_matcher_matrix(key, part):
    common = temporal_common(key)
    return common.astype(jnp.bfloat16)


def draw_within_frame_upstream_derivative(key, part):
    key = jax.random.fold_in(key, 7)
    full_shape = (CLIPS, FRAMES, PATCHES, SHARD_CHANNELS * K)
    return (clipped_normal(key, full_shape) * rising_scale()).astype(jnp.bfloat16)


def draw_across_time_upstream_derivative(key, part):
    key = jax.random.fold_in(key, 9)
    full_shape = (CLIPS, FRAMES, PATCHES, SHARD_CHANNELS * K)
    return (clipped_normal(key, full_shape) * rising_scale()).astype(jnp.bfloat16)


def levels(stream_key, extent, pieces, low, top_value):
    def one(axis_at, shards_of):
        steps = jax.random.uniform(jax.random.fold_in(jax.random.fold_in(stream_key, 6), axis_at), (shards_of,), jnp.float32, low / len(pieces), top_value / len(pieces))
        return jnp.repeat(jnp.exp(steps), extent[axis_at] // shards_of).reshape((-1,) + (1,) * (len(extent) - axis_at - 1))

    loudness = one(*pieces[0])
    for cut in pieces[1:]:
        loudness = loudness * one(*cut)
    return loudness


def normal_values(key, shape, scale, bound, cuts=(), kind=jnp.bfloat16):
    gain = levels(key, shape, cuts, -0.22, 0.18) if cuts else 1.0
    values = jax.random.normal(key, shape, jnp.float32) * scale * gain
    return jnp.minimum(jnp.maximum(values, -bound), bound).astype(kind)


def setup_inputs(seed: int = 0) -> dict:
    key_of = jax.random.split(jax.random.key(seed), 10)
    return {
        "within_frame_asker_matrix": draw_within_frame_asker_matrix(jax.random.fold_in(key_of[9], 71), 0),
        "within_frame_matcher_matrix": draw_within_frame_matcher_matrix(jax.random.fold_in(key_of[9], 71), 0),
        "within_frame_payload_matrix": normal_values(key_of[2], (CLIPS, FRAMES, PATCHES, SHARD_CHANNELS * K), 1.0, 5.0, ((0, 32), (1, 16))),
        "within_frame_upstream_derivative": draw_within_frame_upstream_derivative(jax.random.fold_in(key_of[9], 71), 0),
        "across_time_asker_matrix": draw_across_time_asker_matrix(jax.random.fold_in(key_of[9], 71), 0),
        "across_time_matcher_matrix": draw_across_time_matcher_matrix(jax.random.fold_in(key_of[9], 71), 0),
        "across_time_payload_matrix": normal_values(key_of[6], (CLIPS, FRAMES, PATCHES, SHARD_CHANNELS * K), 1.0, 5.0, ((0, 32), (1, 16))),
        "across_time_upstream_derivative": draw_across_time_upstream_derivative(jax.random.fold_in(key_of[9], 71), 0),
        "sharpness_factor": jnp.clip(jnp.exp(jax.random.uniform(key_of[8], (2, SHARD_CHANNELS), jnp.float32, math.log(0.7), math.log(1.4))), 0.7, 1.4),
    }


def softmax_mixing_reverse_pass(queries, key_rows, values, cotangent, temper_row, causal):
    head_width = queries.shape[-1]
    queries_f = queries.astype(jnp.float32)
    keys_f = key_rows.astype(jnp.float32)
    values_f = values.astype(jnp.float32)
    cotangent_f = cotangent.astype(jnp.float32)
    raw_scores = jnp.einsum('lbhk,mbhk->bhlm', queries_f, keys_f) / math.sqrt(head_width)
    scores = temper_row[None, :, None, None] * raw_scores
    if causal:
        length = queries.shape[0]
        row_index = lax.broadcasted_iota(jnp.int32, (length, length), 0)
        col_index = lax.broadcasted_iota(jnp.int32, (length, length), 1)
        scores = jnp.where(col_index <= row_index, scores, -jnp.inf)
    row_max = lax.optimization_barrier(jnp.max(scores, axis=-1, keepdims=True))
    exponent = jnp.exp(scores - row_max)
    soft_weights = exponent / lax.optimization_barrier(jnp.sum(exponent, axis=-1, keepdims=True))
    weights_low = lax.optimization_barrier(soft_weights.astype(jnp.bfloat16)).astype(jnp.float32)
    value_grad = jnp.einsum('bhlm,lbhk->mbhk', weights_low, cotangent_f)
    weight_grad = jnp.einsum('lbhk,mbhk->bhlm', cotangent_f, values_f)
    row_delta = lax.optimization_barrier(jnp.sum(soft_weights * weight_grad, axis=-1, keepdims=True))
    score_grad = soft_weights * (weight_grad - row_delta)
    score_low = lax.optimization_barrier(score_grad.astype(jnp.bfloat16)).astype(jnp.float32)
    factor = (temper_row / math.sqrt(head_width))[None, None, :, None]
    query_grad = jnp.einsum('bhlm,mbhk->lbhk', score_low, keys_f) * factor
    key_grad = jnp.einsum('bhlm,lbhk->mbhk', score_low, queries_f) * factor
    payload_derivative_share = lax.optimization_barrier(jnp.sum(score_grad * raw_scores, axis=(2, 3)))
    return (query_grad.astype(jnp.bfloat16), key_grad.astype(jnp.bfloat16), value_grad.astype(jnp.bfloat16), payload_derivative_share)

def reference(within_frame_asker_matrix, within_frame_matcher_matrix, within_frame_payload_matrix, within_frame_upstream_derivative, across_time_asker_matrix, across_time_matcher_matrix, across_time_payload_matrix, across_time_upstream_derivative, sharpness_factor):
    clips, frames, patches, features = within_frame_asker_matrix.shape
    channel_bundle = sharpness_factor.shape[1]
    head_width = features // channel_bundle

    def spatial_block(layer_sequence):
        return softmax_mixing_reverse_pass(layer_sequence[0], layer_sequence[1], layer_sequence[2], layer_sequence[3], sharpness_factor[0], False)

    def temporal_block(layer_sequence):
        return softmax_mixing_reverse_pass(layer_sequence[0], layer_sequence[1], layer_sequence[2], layer_sequence[3], sharpness_factor[1], True)
    spatial_in = tuple((block.reshape(clips * frames, patches, 1, channel_bundle, head_width) for block in (within_frame_asker_matrix, within_frame_matcher_matrix, within_frame_payload_matrix, within_frame_upstream_derivative)))
    spatial_result = lax.map(spatial_block, spatial_in)
    temporal_in = tuple((block.reshape(clips, frames, patches, channel_bundle, head_width) for block in (across_time_asker_matrix, across_time_matcher_matrix, across_time_payload_matrix, across_time_upstream_derivative)))
    temporal_result = lax.map(temporal_block, temporal_in)
    scale_norm = 1.0 / math.sqrt(clips * frames * patches)
    logit_scale_gradient = jnp.stack([lax.optimization_barrier(jnp.sum(spatial_result[3], axis=(0, 1))), lax.optimization_barrier(jnp.sum(temporal_result[3], axis=(0, 1)))]) * scale_norm
    entire_result = (clips, frames, patches, features)
    return (spatial_result[0].reshape(entire_result), spatial_result[1].reshape(entire_result), temporal_result[0].reshape(entire_result), temporal_result[1].reshape(entire_result), temporal_result[2].reshape(entire_result), logit_scale_gradient)
```

```python
import functools
import math

import jax
import jax.numpy as jnp
from jax import lax
from jax.experimental import pallas as pl
from jax.experimental.pallas import tpu as pltpu
from jax.sharding import PartitionSpec as P

LANES = 128


def dot(a, b, a_dim, b_dim):
    return lax.dot_general(
        a, b, (((a_dim,), (b_dim,)), ((), ())), preferred_element_type=jnp.float32
    )


def head_gradients(queries, keys, values, cotangent, sharpness, allowed):
    inverse_root = 1.0 / math.sqrt(queries.shape[1])
    raw = dot(keys, queries, 1, 1) * inverse_root
    scores = sharpness * raw
    if allowed is not None:
        scores = jnp.where(allowed, scores, -jnp.inf)
    exponent = jnp.exp(scores - jnp.max(scores, axis=0, keepdims=True))
    weights = exponent * (1.0 / jnp.sum(exponent, axis=0, keepdims=True))
    weight_grad = dot(values, cotangent, 1, 1)
    delta = jnp.sum(weights * weight_grad, axis=0, keepdims=True)
    score_grad = weights * (weight_grad - delta)
    share = jnp.sum(jnp.sum(score_grad * raw, axis=0, keepdims=True), axis=1, keepdims=True)
    score_low = score_grad.astype(jnp.bfloat16)
    factor = sharpness * inverse_root
    query_grad = dot(score_low, keys, 0, 0) * factor
    key_grad = dot(score_low, queries, 1, 0) * factor
    return query_grad, key_grad, weights.astype(jnp.bfloat16), share


def spatial_kernel(heads, sharpness_ref, q_ref, k_ref, v_ref, g_ref, dq_ref, dk_ref, share_ref):
    lane = lax.broadcasted_iota(jnp.int32, (1, LANES), 1)
    shares = jnp.zeros((1, LANES), jnp.float32)
    width = q_ref.shape[1] // heads
    for h in range(heads):
        cols = slice(h * width, (h + 1) * width)
        dq, dk, _, share = head_gradients(
            q_ref[:, cols], k_ref[:, cols], v_ref[:, cols], g_ref[:, cols], sharpness_ref[0, h], None
        )
        dq_ref[:, cols] = dq.astype(jnp.bfloat16)
        dk_ref[:, cols] = dk.astype(jnp.bfloat16)
        shares = jnp.where(lane == h, share, shares)
    share_ref[...] = shares


def temporal_kernel(heads, group_width, sharpness_ref, share_ref, x_ref, out_ref):
    rows = x_ref.shape[0]
    features = x_ref.shape[1] // 4
    width = features // heads
    key_row = lax.broadcasted_iota(jnp.int32, (rows, rows), 0)
    query_row = lax.broadcasted_iota(jnp.int32, (rows, rows), 1)
    allowed = (key_row % group_width == query_row % group_width) & (key_row <= query_row)
    lane = lax.broadcasted_iota(jnp.int32, (1, LANES), 1)
    shares = share_ref[...]
    for h in range(heads):
        q, k, v, g = (
            x_ref[:, part * features + h * width : part * features + (h + 1) * width]
            for part in range(4)
        )
        dq, dk, weights_low, share = head_gradients(q, k, v, g, sharpness_ref[1, h], allowed)
        dv = dot(weights_low, g, 1, 0)
        for part, grad in enumerate((dq, dk, dv)):
            start = part * features + h * width
            out_ref[:, start : start + width] = grad.astype(jnp.bfloat16)
        shares = jnp.where(lane == heads + h, share, shares)
    high = shares.astype(jnp.bfloat16).astype(jnp.float32)
    middle = (shares - high).astype(jnp.bfloat16).astype(jnp.float32)
    low = shares - high - middle
    place = lax.broadcasted_iota(jnp.int32, (rows, LANES), 0) % group_width
    pieces = jnp.where(
        place == 0, high, jnp.where(place == 1, middle, jnp.where(place == 2, low, 0.0))
    )
    out_ref[:, 3 * features :] = pieces.astype(jnp.bfloat16)


def kernel_cost(rows, features, heads, dots, arrays):
    return pl.CostEstimate(
        flops=2 * dots * rows * rows * features,
        bytes_accessed=2 * arrays * rows * features,
        transcendentals=heads * rows * rows,
    )


def on_device(sq, sk, sv, sg, tq, tk, tv, tg, sharpness):
    heads = sharpness.shape[1]
    patches, features = sq.shape[2:]
    frames = lax.axis_size("frame")
    clips = lax.axis_size("clip")
    group_width = patches // frames
    rows = frames * group_width
    smem = pl.BlockSpec(memory_space=pltpu.SMEM)
    vmem = pl.BlockSpec(memory_space=pltpu.VMEM)

    sent = jnp.concatenate(
        [a.reshape(frames, group_width, features) for a in (tq, tk, tv, tg)], axis=2
    )
    arrived = lax.all_to_all(sent, "frame", split_axis=0, concat_axis=0, tiled=True)

    spatial_q, spatial_k, shares = pl.pallas_call(
        functools.partial(spatial_kernel, heads),
        out_shape=(
            jax.ShapeDtypeStruct((patches, features), jnp.bfloat16),
            jax.ShapeDtypeStruct((patches, features), jnp.bfloat16),
            jax.ShapeDtypeStruct((1, LANES), jnp.float32),
        ),
        in_specs=[smem, vmem, vmem, vmem, vmem],
        out_specs=(vmem, vmem, vmem),
        cost_estimate=kernel_cost(patches, features, heads, 4, 6),
        name="spatial",
    )(sharpness, *(a.reshape(patches, features) for a in (sq, sk, sv, sg)))

    grads = pl.pallas_call(
        functools.partial(temporal_kernel, heads, group_width),
        out_shape=jax.ShapeDtypeStruct((rows, 3 * features + LANES), jnp.bfloat16),
        in_specs=[smem, vmem, vmem],
        out_specs=vmem,
        cost_estimate=kernel_cost(rows, features, heads, 5, 7),
        name="temporal",
    )(sharpness, shares, arrived.reshape(rows, 4 * features))

    back = lax.all_to_all(
        grads.reshape(frames, group_width, 3 * features + LANES),
        "frame",
        split_axis=0,
        concat_axis=0,
        tiled=True,
    )
    frame_sum = jnp.sum(back[:, :, 3 * features :].astype(jnp.float32), axis=(0, 1))
    everyone = lax.all_to_all(
        jnp.broadcast_to(frame_sum[None, None], (clips, 1, LANES)),
        "clip",
        split_axis=0,
        concat_axis=0,
        tiled=True,
    )
    scale_norm = 1.0 / math.sqrt(clips * sq.shape[0] * frames * sq.shape[1] * patches)
    total = jnp.sum(everyone, axis=(0, 1)) * scale_norm

    def whole(block):
        return block.reshape(1, 1, patches, features)

    return (
        whole(spatial_q),
        whole(spatial_k),
        whole(back[:, :, :features]),
        whole(back[:, :, features : 2 * features]),
        whole(back[:, :, 2 * features : 3 * features]),
        total[: 2 * heads].reshape(2, heads),
    )


def solution(mesh):
    split = P("clip", "frame", None, None)
    return jax.shard_map(
        on_device,
        mesh=mesh,
        in_specs=(split,) * 8 + (P(),),
        out_specs=(split,) * 5 + (P(),),
        check_vma=False,
    )
```

```python
import functools
import math

import jax
import jax.numpy as jnp
from jax import lax
from jax.experimental import pallas as pl
from jax.experimental.pallas import tpu as pltpu
from jax.sharding import PartitionSpec as P

LANES = 128
BUNDLE = 12
PACK_PIECES = 4
VMEM_BYTES = 16 * 2**20


def dot(a, b, a_dim, b_dim):
    return lax.dot_general(
        a, b, (((a_dim,), (b_dim,)), ((), ())), preferred_element_type=jnp.float32
    )


def score_gradients(raw, weight_grad, sharpness, allowed):
    scores = sharpness * raw
    if allowed is not None:
        scores = jnp.where(allowed, scores, -jnp.inf)
    exponent = jnp.exp(scores - jnp.max(scores, axis=0, keepdims=True))
    weights = exponent * (1.0 / jnp.sum(exponent, axis=0, keepdims=True))
    delta = jnp.sum(weights * weight_grad, axis=0, keepdims=True)
    score_grad = weights * (weight_grad - delta)
    share = jnp.sum(score_grad * raw, axis=0, keepdims=True)
    return weights, score_grad, share


def bundle_gradients(loads, sharpness, allowed, with_values):
    heads = [load() for load in loads]
    inverse_root = 1.0 / math.sqrt(heads[0][0].shape[1])
    raws = [dot(k, q, 1, 1) for q, k, v, g in heads]
    weight_grads = [dot(v, g, 1, 1) for q, k, v, g in heads]
    parts = [
        score_gradients(raw, weight_grad, sharp * inverse_root, allowed)
        for raw, weight_grad, sharp in zip(raws, weight_grads, sharpness)
    ]
    outs = []
    for (q, k, v, g), (weights, score_grad, share), sharp in zip(heads, parts, sharpness):
        score_low = score_grad.astype(jnp.bfloat16)
        factor = sharp * inverse_root
        grads = [dot(score_low, k, 0, 0) * factor, dot(score_low, q, 1, 0) * factor]
        if with_values:
            grads.append(dot(weights.astype(jnp.bfloat16), g, 1, 0))
        total = jnp.sum(share, axis=1, keepdims=True) * inverse_root
        outs.append(([grad.astype(jnp.bfloat16) for grad in grads], total))
    return outs


def spatial_kernel(heads, sharpness_ref, q_ref, k_ref, v_ref, g_ref, dq_ref, dk_ref, share_ref):
    lane = lax.broadcasted_iota(jnp.int32, (1, LANES), 1)
    shares = jnp.zeros((1, LANES), jnp.float32)
    width = q_ref.shape[1] // heads
    for first in range(0, heads, BUNDLE):
        bundle = range(first, min(first + BUNDLE, heads))
        columns = [slice(h * width, (h + 1) * width) for h in bundle]
        loads = [
            lambda cols=cols: [ref[:, cols] for ref in (q_ref, k_ref, v_ref, g_ref)]
            for cols in columns
        ]
        outs = bundle_gradients(loads, [sharpness_ref[0, h] for h in bundle], None, False)
        for h, cols, ((dq, dk), share) in zip(bundle, columns, outs):
            dq_ref[:, cols] = dq
            dk_ref[:, cols] = dk
            shares = jnp.where(lane == h, share, shares)
    share_ref[...] = shares


def temporal_kernel(heads, group_width, first_frame, sharpness_ref, share_ref, x_ref, out_ref):
    rows = x_ref.shape[0]
    features = x_ref.shape[1] // 4
    width = features // heads
    key_row = lax.broadcasted_iota(jnp.int32, (rows, rows), 0)
    query_row = lax.broadcasted_iota(jnp.int32, (rows, rows), 1)
    key_frame, query_frame = (
        (row // group_width + first_frame) % (rows // group_width) for row in (key_row, query_row)
    )
    allowed = (key_row % group_width == query_row % group_width) & (key_frame <= query_frame)
    lane = lax.broadcasted_iota(jnp.int32, (1, LANES), 1)
    shares = share_ref[...]

    def columns(part, h):
        return slice(part * features + h * width, part * features + (h + 1) * width)

    for first in range(0, heads, BUNDLE):
        bundle = range(first, min(first + BUNDLE, heads))
        loads = [lambda h=h: [x_ref[:, columns(part, h)] for part in range(4)] for h in bundle]
        outs = bundle_gradients(loads, [sharpness_ref[1, h] for h in bundle], allowed, True)
        for h, (grads, share) in zip(bundle, outs):
            for part, grad in enumerate(grads):
                out_ref[:, columns(part, h)] = grad
            shares = jnp.where(lane == heads + h, share, shares)
    high = shares.astype(jnp.bfloat16).astype(jnp.float32)
    middle = (shares - high).astype(jnp.bfloat16).astype(jnp.float32)
    low = shares - high - middle
    place = lax.broadcasted_iota(jnp.int32, (rows, LANES), 0) % group_width
    pieces = jnp.where(
        place == 0, high, jnp.where(place == 1, middle, jnp.where(place == 2, low, 0.0))
    )
    out_ref[:, 3 * features :] = pieces.astype(jnp.bfloat16)


def pack_kernel(q_ref, k_ref, v_ref, g_ref, out_ref, staged_ref, in_sems, out_sems):
    rows, features = q_ref.shape
    step = rows // PACK_PIECES
    pieces = [slice(piece * step, (piece + 1) * step) for piece in range(PACK_PIECES)]
    arriving = [
        [
            pltpu.make_async_copy(
                ref.at[piece],
                staged_ref.at[piece, part * features : (part + 1) * features],
                in_sems.at[part, i],
            )
            for part, ref in enumerate((q_ref, k_ref, v_ref, g_ref))
        ]
        for i, piece in enumerate(pieces)
    ]
    leaving = [
        pltpu.make_async_copy(staged_ref.at[piece], out_ref.at[piece], out_sems.at[i])
        for i, piece in enumerate(pieces)
    ]
    for copies in arriving:
        for copy in copies:
            copy.start()
    for copies, copy_out in zip(arriving, leaving):
        for copy in copies:
            copy.wait()
        copy_out.start()
    for copy_out in leaving:
        copy_out.wait()


def kernel_cost(rows, features, heads, dots, arrays):
    return pl.CostEstimate(
        flops=2 * dots * rows * rows * features,
        bytes_accessed=2 * arrays * rows * features,
        transcendentals=heads * rows * rows,
    )


def on_device(sq, sk, sv, sg, tq, tk, tv, tg, sharpness):
    heads = sharpness.shape[1]
    patches, features = sq.shape[2:]
    frames = lax.axis_size("frame")
    clips = lax.axis_size("clip")
    group_width = patches // frames
    rows = frames * group_width
    first_frame = frames // 2
    frame_groups = [[(i + first_frame) % frames for i in range(frames)]]
    clip_groups = [[(i + 3 * clips // 4) % clips for i in range(clips)]]
    smem = pl.BlockSpec(memory_space=pltpu.SMEM)
    vmem = pl.BlockSpec(memory_space=pltpu.VMEM)

    params = pltpu.CompilerParams(vmem_limit_bytes=VMEM_BYTES)
    hbm = pl.BlockSpec(memory_space=pltpu.HBM)
    sent = pl.pallas_call(
        pack_kernel,
        out_shape=jax.ShapeDtypeStruct((patches, 4 * features), jnp.bfloat16),
        in_specs=[hbm] * 4,
        out_specs=hbm,
        scratch_shapes=[
            pltpu.VMEM((patches, 4 * features), jnp.bfloat16),
            pltpu.SemaphoreType.DMA((4, PACK_PIECES)),
            pltpu.SemaphoreType.DMA((PACK_PIECES,)),
        ],
        cost_estimate=pl.CostEstimate(
            flops=0, bytes_accessed=16 * patches * features, transcendentals=0
        ),
        name="pack",
    )(*(a.reshape(patches, features) for a in (tq, tk, tv, tg)))
    arrived = lax.all_to_all(
        sent.reshape(frames, group_width, 4 * features),
        "frame",
        split_axis=0,
        concat_axis=0,
        axis_index_groups=frame_groups,
        tiled=True,
    )

    spatial_q, spatial_k, shares = pl.pallas_call(
        functools.partial(spatial_kernel, heads),
        out_shape=(
            jax.ShapeDtypeStruct((patches, features), jnp.bfloat16),
            jax.ShapeDtypeStruct((patches, features), jnp.bfloat16),
            jax.ShapeDtypeStruct((1, LANES), jnp.float32),
        ),
        in_specs=[smem, vmem, vmem, vmem, vmem],
        out_specs=(vmem, vmem, vmem),
        compiler_params=params,
        cost_estimate=kernel_cost(patches, features, heads, 4, 6),
        name="spatial",
    )(sharpness, *(a.reshape(patches, features) for a in (sq, sk, sv, sg)))

    grads = pl.pallas_call(
        functools.partial(temporal_kernel, heads, group_width, first_frame),
        out_shape=jax.ShapeDtypeStruct((rows, 3 * features + LANES), jnp.bfloat16),
        in_specs=[smem, vmem, vmem],
        out_specs=vmem,
        compiler_params=params,
        cost_estimate=kernel_cost(rows, features, heads, 5, 7),
        name="temporal",
    )(sharpness, shares, arrived.reshape(rows, 4 * features))

    back = lax.all_to_all(
        grads.reshape(frames, group_width, 3 * features + LANES),
        "frame",
        split_axis=0,
        concat_axis=0,
        axis_index_groups=frame_groups,
        tiled=True,
    )
    frame_sum = jnp.sum(back[:, :, 3 * features :].astype(jnp.float32), axis=(0, 1))
    everyone = lax.all_to_all(
        jnp.broadcast_to(frame_sum[None, None], (clips, 1, LANES)),
        "clip",
        split_axis=0,
        concat_axis=0,
        axis_index_groups=clip_groups,
        tiled=True,
    )
    scale_norm = 1.0 / math.sqrt(clips * sq.shape[0] * frames * sq.shape[1] * patches)
    total = jnp.sum(everyone, axis=(0, 1)) * scale_norm

    def whole(block):
        return block.reshape(1, 1, patches, features)

    return (
        whole(spatial_q),
        whole(spatial_k),
        whole(back[:, :, :features]),
        whole(back[:, :, features : 2 * features]),
        whole(back[:, :, 2 * features : 3 * features]),
        total[: 2 * heads].reshape(2, heads),
    )


def solution(mesh):
    split = P("clip", "frame", None, None)
    return jax.shard_map(
        on_device,
        mesh=mesh,
        in_specs=(split,) * 8 + (P(),),
        out_specs=(split,) * 5 + (P(),),
        check_vma=False,
    )
```

```python
import functools
import math

import jax
import jax.numpy as jnp
from jax import lax
from jax.experimental import pallas as pl
from jax.experimental.pallas import tpu as pltpu
from jax.sharding import PartitionSpec as P

LANES = 128
BUNDLE = 12
VMEM_BYTES = 16 * 2**20


def dot(a, b, a_dim, b_dim):
    return lax.dot_general(
        a, b, (((a_dim,), (b_dim,)), ((), ())), preferred_element_type=jnp.float32
    )


def score_gradients(raw, weight_grad, sharpness, hidden):
    scores = sharpness * raw
    if hidden is not None:
        scores = scores + hidden
    exponent = jnp.exp(scores - jnp.max(scores, axis=0, keepdims=True))
    weights = exponent * (1.0 / jnp.sum(exponent, axis=0, keepdims=True))
    delta = jnp.sum(weights * weight_grad, axis=0, keepdims=True)
    score_grad = weights * (weight_grad - delta)
    share = jnp.sum(score_grad * raw, axis=0, keepdims=True)
    return weights, score_grad, share


def bundle_gradients(loads, sharpness, hidden, with_values):
    heads = [load() for load in loads]
    inverse_root = 1.0 / math.sqrt(heads[0][0].shape[1])
    raws = [dot(k, q, 1, 1) for q, k, v, g in heads]
    weight_grads = [dot(v, g, 1, 1) for q, k, v, g in heads]
    parts = [
        score_gradients(raw, weight_grad, sharp * inverse_root, hidden)
        for raw, weight_grad, sharp in zip(raws, weight_grads, sharpness)
    ]
    outs = []
    for (q, k, v, g), (weights, score_grad, share), sharp in zip(heads, parts, sharpness):
        score_low = score_grad.astype(jnp.bfloat16)
        factor = sharp * inverse_root
        grads = [dot(score_low, k, 0, 0) * factor, dot(score_low, q, 1, 0) * factor]
        if with_values:
            grads.append(dot(weights.astype(jnp.bfloat16), g, 1, 0))
        total = jnp.sum(share, axis=1, keepdims=True) * inverse_root
        outs.append(([grad.astype(jnp.bfloat16) for grad in grads], total))
    return outs


def spatial_kernel(heads, sharpness_ref, q_ref, k_ref, v_ref, g_ref, dq_ref, dk_ref, share_ref):
    lane = lax.broadcasted_iota(jnp.int32, (1, LANES), 1)
    shares = jnp.zeros((1, LANES), jnp.float32)
    width = q_ref.shape[1] // heads
    for first in range(0, heads, BUNDLE):
        bundle = range(first, min(first + BUNDLE, heads))
        columns = [slice(h * width, (h + 1) * width) for h in bundle]
        loads = [
            lambda cols=cols: [ref[:, cols] for ref in (q_ref, k_ref, v_ref, g_ref)]
            for cols in columns
        ]
        outs = bundle_gradients(loads, [sharpness_ref[0, h] for h in bundle], None, False)
        for h, cols, ((dq, dk), share) in zip(bundle, columns, outs):
            dq_ref[:, cols] = dq
            dk_ref[:, cols] = dk
            shares = jnp.where(lane == h, share, shares)
    share_ref[...] = shares


def temporal_kernel(heads, group_width, first_frame, sharpness_ref, share_ref, x_ref, out_ref):
    rows = x_ref.shape[0]
    features = x_ref.shape[1] // 4
    width = features // heads
    key_row = lax.broadcasted_iota(jnp.int32, (rows, rows), 0)
    query_row = lax.broadcasted_iota(jnp.int32, (rows, rows), 1)
    key_frame, query_frame = (
        (row // group_width + first_frame) % (rows // group_width) for row in (key_row, query_row)
    )
    allowed = (key_row % group_width == query_row % group_width) & (key_frame <= query_frame)
    hidden = jnp.where(allowed, 0.0, -jnp.inf)
    lane = lax.broadcasted_iota(jnp.int32, (1, LANES), 1)
    shares = share_ref[...]

    def columns(part, h):
        return slice(part * features + h * width, part * features + (h + 1) * width)

    for first in range(0, heads, BUNDLE):
        bundle = range(first, min(first + BUNDLE, heads))
        loads = [lambda h=h: [x_ref[:, columns(part, h)] for part in range(4)] for h in bundle]
        outs = bundle_gradients(loads, [sharpness_ref[1, h] for h in bundle], hidden, True)
        for h, (grads, share) in zip(bundle, outs):
            for part, grad in enumerate(grads):
                out_ref[:, columns(part, h)] = grad
            shares = jnp.where(lane == heads + h, share, shares)
    high = shares.astype(jnp.bfloat16).astype(jnp.float32)
    middle = (shares - high).astype(jnp.bfloat16).astype(jnp.float32)
    low = shares - high - middle
    place = lax.broadcasted_iota(jnp.int32, (rows, LANES), 0) % group_width
    pieces = jnp.where(
        place == 0, high, jnp.where(place == 1, middle, jnp.where(place == 2, low, 0.0))
    )
    out_ref[:, 3 * features :] = pieces.astype(jnp.bfloat16)


def pack_kernel(q_ref, k_ref, v_ref, g_ref, out_ref, staged_ref, in_sems, out_sems):
    features = q_ref.shape[1]
    arriving = [
        pltpu.make_async_copy(ref, staged_ref.at[part], in_sems.at[part])
        for part, ref in enumerate((q_ref, k_ref, v_ref, g_ref))
    ]
    leaving = [
        pltpu.make_async_copy(
            staged_ref.at[part],
            out_ref.at[:, part * features : (part + 1) * features],
            out_sems.at[part],
        )
        for part in range(4)
    ]
    for copy in arriving:
        copy.start()
    for copy, copy_out in zip(arriving, leaving):
        copy.wait()
        copy_out.start()
    for copy_out in leaving:
        copy_out.wait()


def kernel_cost(rows, features, heads, dots, arrays):
    return pl.CostEstimate(
        flops=2 * dots * rows * rows * features,
        bytes_accessed=2 * arrays * rows * features,
        transcendentals=heads * rows * rows,
    )


def on_device(sq, sk, sv, sg, tq, tk, tv, tg, sharpness):
    heads = sharpness.shape[1]
    patches, features = sq.shape[2:]
    frames = lax.axis_size("frame")
    clips = lax.axis_size("clip")
    group_width = patches // frames
    rows = frames * group_width
    first_frame = frames // 2
    frame_groups = [[(i + first_frame) % frames for i in range(frames)]]
    clip_order = [(i + 3 * clips // 4) % clips for i in range(clips)]
    clip_groups = [
        [(f ^ 2 if c >= clips // 2 else f) * clips + c for c in clip_order] for f in range(frames)
    ]
    smem = pl.BlockSpec(memory_space=pltpu.SMEM)
    vmem = pl.BlockSpec(memory_space=pltpu.VMEM)

    params = pltpu.CompilerParams(vmem_limit_bytes=VMEM_BYTES)
    hbm = pl.BlockSpec(memory_space=pltpu.HBM)
    sent = pl.pallas_call(
        pack_kernel,
        out_shape=jax.ShapeDtypeStruct((patches, 4 * features), jnp.bfloat16),
        in_specs=[hbm] * 4,
        out_specs=hbm,
        scratch_shapes=[
            pltpu.VMEM((4, patches, features), jnp.bfloat16),
            pltpu.SemaphoreType.DMA((4,)),
            pltpu.SemaphoreType.DMA((4,)),
        ],
        cost_estimate=pl.CostEstimate(
            flops=0, bytes_accessed=16 * patches * features, transcendentals=0
        ),
        name="pack",
    )(*(a.reshape(patches, features) for a in (tq, tk, tv, tg)))
    arrived = lax.all_to_all(
        sent.reshape(frames, group_width, 4 * features),
        "frame",
        split_axis=0,
        concat_axis=0,
        axis_index_groups=frame_groups,
        tiled=True,
    )

    spatial_q, spatial_k, shares = pl.pallas_call(
        functools.partial(spatial_kernel, heads),
        out_shape=(
            jax.ShapeDtypeStruct((patches, features), jnp.bfloat16),
            jax.ShapeDtypeStruct((patches, features), jnp.bfloat16),
            jax.ShapeDtypeStruct((1, LANES), jnp.float32),
        ),
        in_specs=[smem, vmem, vmem, vmem, vmem],
        out_specs=(vmem, vmem, vmem),
        compiler_params=params,
        cost_estimate=kernel_cost(patches, features, heads, 4, 6),
        name="spatial",
    )(sharpness, *(a.reshape(patches, features) for a in (sq, sk, sv, sg)))

    grads = pl.pallas_call(
        functools.partial(temporal_kernel, heads, group_width, first_frame),
        out_shape=jax.ShapeDtypeStruct((rows, 3 * features + LANES), jnp.bfloat16),
        in_specs=[smem, vmem, vmem],
        out_specs=vmem,
        compiler_params=params,
        cost_estimate=kernel_cost(rows, features, heads, 5, 7),
        name="temporal",
    )(sharpness, shares, arrived.reshape(rows, 4 * features))

    back = lax.all_to_all(
        grads.reshape(frames, group_width, 3 * features + LANES),
        "frame",
        split_axis=0,
        concat_axis=0,
        axis_index_groups=frame_groups,
        tiled=True,
    )
    frame_sum = jnp.sum(back[:, :, 3 * features :].astype(jnp.float32), axis=(0, 1))
    everyone = lax.all_to_all(
        jnp.broadcast_to(frame_sum[None, None], (clips, 1, LANES)),
        ("frame", "clip"),
        split_axis=0,
        concat_axis=0,
        axis_index_groups=clip_groups,
        tiled=True,
    )
    scale_norm = 1.0 / math.sqrt(clips * sq.shape[0] * frames * sq.shape[1] * patches)
    total = jnp.sum(everyone, axis=(0, 1)) * scale_norm

    def whole(block):
        return block.reshape(1, 1, patches, features)

    return (
        whole(spatial_q),
        whole(spatial_k),
        whole(back[:, :, :features]),
        whole(back[:, :, features : 2 * features]),
        whole(back[:, :, 2 * features : 3 * features]),
        total[: 2 * heads].reshape(2, heads),
    )


def solution(mesh):
    split = P("clip", "frame", None, None)
    return jax.shard_map(
        on_device,
        mesh=mesh,
        in_specs=(split,) * 8 + (P(),),
        out_specs=(split,) * 5 + (P(),),
        check_vma=False,
    )
```
